128 devices in a mesh: row: 8 (over z, y_hi), col: 16 (over x, y_lo, core).
Axes of the slice: x: 4, y: 4 (y_hi: 2, y_lo: 2; y = y_hi * 2 + y_lo), z: 4, core: 2. Of those that a mesh axis runs over, the one named last changes fastest.
Arguments:
- a_panels: bfloat16 [16384, 32768], P('row', 'col'), may hold values from -6 to 6
- a_flags: int32 [256, 512], P('row', 'col'), may hold values 0 or 1
- b_panels: bfloat16 [32768, 8192], P('row', 'col'), may hold values from -0.09375 to 0.09375
- b_flags: int32 [512, 128], P('row', 'col'), may hold values 0 or 1
Outputs:
- product: float32 [16384, 8192], P('row', 'col')
The draws below stay inside these ranges and needn't reach their ends.
All inputs are finite; a program needn't handle non-finite values. No bound on the sum of `a_flags` or of `b_flags` on one device may be relied on, other than what follows from the above.
Results may differ from the reference program's by a relative error of at most 0.0003.
Values may be sent and summed in bfloat16 or wider, within the bound.
A program may use at most 128 MiB of HBM per device.

```python
import jax
import jax.numpy as jnp
from jax import lax

BS = 64
RB_DEV = 32
KB = 32
CB_DEV = 8
STEPS = 4
ROWS = 16384
COLS = 8192
AK = 32768
BK = 32768
N_ROW = 8
N_COL = 16


def plant(array, own_key, low, high):
    longest = array.shape.index(max(array.shape))
    spots = []
    for shift in (0, 1):
        where = [jax.random.randint(jax.random.fold_in(own_key, axis), (), 0, length) for axis, length in enumerate(array.shape)]
        where[longest] = (where[longest] + shift) % array.shape[longest]
        spots.append(tuple(where))
    return array.at[spots[0]].set(low).at[spots[1]].set(high)


def block_levels(rng, dims, shards, low, largest):
    level, own = 1.0, jax.random.fold_in(rng, 6)
    for dim, parts in shards:
        draws = jnp.exp(jax.random.uniform(jax.random.fold_in(own, dim), (parts,), jnp.float32, low / len(shards), largest / len(shards)))
        level = level * jnp.repeat(draws, dims[dim] // parts).reshape([-1 if axis == dim else 1 for axis in range(len(dims))])
    return level


def normal_values(own_key, extent, spread, bound, cuts=(), dtype=jnp.bfloat16):
    values = spread * jax.random.normal(own_key, extent, jnp.float32)
    if cuts:
        values = values * block_levels(own_key, extent, cuts, -0.22, 0.18)
    return jnp.clip(values, -bound, bound).astype(dtype)


def setup_inputs(seed: int = 0) -> dict:
    splits = jax.random.split(jax.random.key(seed), 5)
    return {
        "a_panels": normal_values(splits[0], (ROWS, AK), 1.0, 6.0, ((0, 8), (1, 16))),
        "a_flags": plant((jax.random.randint(splits[1], (RB_DEV * N_ROW, KB * N_COL), 0, 2) < 1).astype(jnp.int32), jax.random.fold_in(splits[1], 1), 0, 1),
        "b_panels": normal_values(splits[2], (BK, COLS), (2 * KB * BS) ** -0.5, 0.09375, ((0, 8), (1, 16))),
        "b_flags": plant((jax.random.randint(splits[3], (2 * KB * N_ROW, CB_DEV * N_COL), 0, 2) < 1).astype(jnp.int32), jax.random.fold_in(splits[3], 1), 0, 1),
    }


def expand(data, flags, blocks_down, blocks_across):
    shaped = data.astype(jnp.float32).reshape(blocks_down, BS, blocks_across, BS)
    masked = shaped * flags.astype(jnp.float32)[:, None, :, None]
    return masked.reshape(blocks_down * BS, blocks_across * BS)


def reference(a_panels, a_flags, b_panels, b_flags):
    left = expand(a_panels, a_flags, RB_DEV * N_ROW, KB * N_COL)
    right = expand(b_panels, b_flags, 2 * KB * N_ROW, CB_DEV * N_COL)
    row_width = RB_DEV * BS
    group_width = KB * BS
    col_width = CB_DEV * BS
    stripes = []
    for i in range(N_ROW):
        pieces = []
        for j in range(N_COL):
            total = jnp.zeros((row_width, col_width), jnp.float32)
            for s in range(STEPS):
                group = (i + j + s) % N_COL
                left_start = ((group - i) % N_COL) * group_width
                left_block = left[i * row_width:(i + 1) * row_width, left_start:left_start + group_width]
                source = (group % N_ROW - j) % N_ROW
                right_start = source * 2 * group_width + (group // N_ROW) * group_width
                right_block = right[right_start:right_start + group_width, j * col_width:(j + 1) * col_width]
                total = total + jnp.dot(left_block, right_block, precision=lax.Precision.HIGHEST)
            pieces.append(total)
        stripes.append(jnp.concatenate(pieces, axis=1))
    return jnp.concatenate(stripes, axis=0)
```

```python
import functools

import jax
import jax.numpy as jnp
from jax import lax
from jax.experimental import pallas as pl
from jax.experimental.pallas import tpu as pltpu
from jax.sharding import PartitionSpec as P

MESH = pl.DeviceIdType.MESH
TILE = 256
HALF = 256
PAD = 16
FINE = 64.0


def lanes_expanded(flags, width):
    count = flags.shape[1]
    owner = lax.broadcasted_iota(jnp.int32, (count, width), 1) // (width // count)
    spread = (owner == lax.broadcasted_iota(jnp.int32, (count, width), 0)).astype(jnp.float32)
    return jnp.dot(flags.astype(jnp.float32), spread, preferred_element_type=jnp.float32)


def coded(value, out_ref):
    rows = value.shape[0]
    largest = jnp.maximum(jnp.max(jnp.abs(value), axis=0, keepdims=True), 1e-30)
    power = jnp.ceil(jnp.log2(largest) * FINE + 0.5)
    scaled = value * (jnp.exp2(power * (-1.0 / FINE)) * 32767.0)
    whole = jnp.round(jnp.clip(scaled, -32767.0, 32767.0))
    out_ref[pl.ds(0, rows), :] = whole.astype(jnp.int32).astype(jnp.int16)
    out_ref[pl.ds(rows, PAD), :] = jnp.broadcast_to(power.astype(jnp.int32), (PAD, value.shape[1])).astype(jnp.int16)


def decoded(in_ref, rows):
    power = in_ref[pl.ds(rows, PAD), :].astype(jnp.int32).astype(jnp.float32)[0:1, :]
    scale = jnp.exp2(power * (1.0 / FINE)) * (1.0 / 32767.0)
    return in_ref[pl.ds(0, rows), :].astype(jnp.int32).astype(jnp.float32) * scale


def kernel(
    n_row, n_col, a_ref, af_ref, b_ref, bf_ref, o_ref,
    left, right, fa, fb, rx, ry, rz, acc, xs, xr, qs, qr, zs, zr,
    a_sem, b_sem, o_sem, send_r, recv_rx, recv_ry, recv_rz,
    send_x, recv_x, send_q, recv_q, send_z, recv_z,
):
    i, j = lax.axis_index("row"), lax.axis_index("col")
    even = lax.rem(j, 2) == 0
    rows, depth = left.shape
    halves, tiles = ry.shape[0], rows // TILE

    def at(di, dj):
        return (lax.rem(i + di + n_row, n_row), lax.rem(j + dj + n_col, n_col))

    def either(e, o):
        return tuple(jnp.where(even, p, q) for p, q in zip(e, o, strict=True))

    def load_a(m):
        part = pl.ds(m * TILE, TILE)
        return pltpu.make_async_copy(a_ref.at[part, :], left.at[part, :], a_sem.at[m])

    def load_b(n):
        return pltpu.make_async_copy(b_ref.at[:, pl.ds(n * HALF, HALF)], right.at[n], b_sem.at[n])

    for n in range(halves):
        load_b(n).start()
    for m in range(tiles):
        load_a(m).start()

    barrier = pltpu.get_barrier_semaphore()

    def greet(where):
        pl.semaphore_signal(barrier, inc=1, device_id=where, device_id_type=MESH)

    greet(either(at(1, -1), at(3, -3)))
    greet(at(2, -2))
    greet(at(0, 2))
    greet(either(at(0, 1), at(0, -1)))

    @pl.when(jnp.logical_not(even))
    def _():
        greet(at(0, 3))

        @pl.when(i != 0)
        def _():
            greet(at(-1, 1))

        @pl.when(i == 0)
        def _():
            greet(at(1, -1))

    @pl.when(jnp.logical_and(even, i == n_row - 1))
    def _():
        greet(at(3, -3))

    fb[...] = lanes_expanded(bf_ref[...], fb.shape[1])
    size_b = b_ref.shape[0] // fb.shape[0]
    fa[...] = lanes_expanded(af_ref[...], depth)
    size_a = rows // fa.shape[0]

    def mask_b(n):
        @pl.loop(0, fb.shape[0])
        def _(k):
            part = pl.ds(pl.multiple_of(k * size_b, size_b), size_b)
            row = fb[pl.ds(k, 1), pl.ds(n * HALF, HALF)].astype(jnp.bfloat16)
            right[n, part, :] = right[n, part, :] * row

    own = lax.rem(i + j, n_col) // n_row

    def half_for(s):
        return lax.rem(own + jnp.where(i < s, 1, 0), 2)

    def block(n, half):
        return right.at[n, pl.ds(pl.multiple_of(half * depth, depth), depth), :]

    def remote(src, dst, ssem, rsem, where):
        return pltpu.make_async_remote_copy(
            src_ref=src, dst_ref=dst, send_sem=ssem, recv_sem=rsem, device_id=where, device_id_type=MESH
        )

    to_x = either(at(-3, 3), at(-1, 1))
    to_y = at(-2, 2)
    to_forward = either(at(1, -1), at(-1, 1))
    to_extra = either(at(-1, 1), at(-3, 3))
    forwards = jnp.where(even, i != n_row - 1, i != 0)
    extra = jnp.where(even, i == 1, i == 2)

    def send_x_block(n):
        half = jnp.where(even, half_for(3), half_for(1))
        return remote(block(n, half), rx.at[n], send_r.at[0, n], recv_rx.at[n], to_x)

    def send_y_block(n):
        return remote(block(n, half_for(2)), ry.at[n], send_r.at[1, n], recv_ry.at[n], to_y)

    def send_extra(n):
        half = jnp.where(even, half_for(1), half_for(3))
        return remote(block(n, half), rz.at[n], send_r.at[3, n], recv_rz.at[n], to_extra)

    def send_forward(n):
        return remote(ry.at[n], rz.at[n], send_r.at[2, n], recv_rz.at[n], to_forward)

    def begin(n):
        send_y_block(n).start()
        send_x_block(n).start()

        @pl.when(extra)
        def _():
            send_extra(n).start()

    load_b(0).wait()
    mask_b(0)
    pl.semaphore_wait(
        barrier, jnp.where(even, 6 + jnp.where(i == 1, 1, 0) - jnp.where(i == n_row - 1, 1, 0), 4 + jnp.where(i == 2, 1, 0))
    )
    begin(0)
    load_b(1).wait()
    mask_b(1)

    @pl.loop(0, tiles)
    def _(m):
        load_a(m).wait()
        for k in range(TILE // size_a):
            part = pl.ds(pl.multiple_of(m * TILE + k * size_a, size_a), size_a)
            row = fa[pl.ds(m * (TILE // size_a) + k, 1), :].astype(jnp.bfloat16)
            left[part, :] = left[part, :] * row

    def product(m, block_ref):
        part = pl.ds(pl.multiple_of(m * TILE, TILE), TILE)
        return jnp.dot(left[part, :], block_ref[...], preferred_element_type=jnp.float32)

    for n in range(halves):
        @pl.loop(0, tiles)
        def _(m):
            acc[n, m] = product(m, block(n, own))

    send_y_block(0).wait_send()
    send_x_block(0).wait_send()
    begin(1)

    partner = either(at(0, 1), at(0, -1))

    def x_copy(n, m):
        return remote(xs.at[n, m], xr.at[n, m], send_x.at[n, m], recv_x.at[n, m], partner)

    def q_copy(n, m):
        return remote(qs.at[n, m], qr.at[n, m], send_q.at[n, m], recv_q.at[n, m], at(0, -2))

    def z_copy(n, m):
        return remote(zs.at[n, m], zr.at[n, m], send_z.at[n, m], recv_z.at[n, m], either(at(0, -3), at(0, -1)))

    for n in range(halves):
        send_y_block(n).wait_recv()

        @pl.when(forwards)
        def _():
            send_forward(n).start()

        send_x_block(n).wait_recv()

        @pl.loop(0, tiles)
        def _(m):
            xs[n, m] = product(m, rx.at[n])
            x_copy(n, m).start()

        @pl.loop(0, tiles)
        def _(m):
            value = product(m, ry.at[n])
            x_copy(n, m).wait_recv()
            coded(value + xr[n, m], qs.at[n, m])
            q_copy(n, m).start()

    for n in range(halves):
        send_forward(n).wait_recv()

        @pl.loop(0, tiles)
        def _(m):
            coded(product(m, rz.at[n]), zs.at[n, m])
            z_copy(n, m).start()

    def store(n, m):
        where = o_ref.at[pl.ds(pl.multiple_of(m * TILE, TILE), TILE), pl.ds(n * HALF, HALF)]
        return pltpu.make_async_copy(acc.at[n, m], where, o_sem.at[n, m])

    for n in range(halves):
        @pl.loop(0, tiles)
        def _(m):
            q_copy(n, m).wait_recv()
            z_copy(n, m).wait_recv()
            acc[n, m] = acc[n, m] + decoded(qr.at[n, m], TILE) + decoded(zr.at[n, m], TILE)
            store(n, m).start()

    for n in range(halves):
        if n > 0:
            send_y_block(n).wait_send()
            send_x_block(n).wait_send()

        @pl.when(forwards)
        def _():
            send_forward(n).wait_send()

        @pl.when(extra)
        def _():
            send_extra(n).wait_send()

        @pl.loop(0, tiles)
        def _(m):
            x_copy(n, m).wait_send()
            q_copy(n, m).wait_send()
            z_copy(n, m).wait_send()
            store(n, m).wait()


def per_device(n_row, n_col, a_panels, a_flags, b_panels, b_flags):
    rows, depth = a_panels.shape
    columns = b_panels.shape[1]
    halves, tiles = columns // HALF, rows // TILE
    bf16, f32, dma = jnp.bfloat16, jnp.float32, pltpu.SemaphoreType.DMA
    taken = pltpu.VMEM((halves, depth, HALF), bf16)
    tile = pltpu.VMEM((halves, tiles, TILE, HALF), f32)
    code = pltpu.VMEM((halves, tiles, TILE + PAD, HALF), jnp.int16)
    each = dma((halves, tiles))
    return pl.pallas_call(
        functools.partial(kernel, n_row, n_col),
        name="block_products",
        out_shape=jax.ShapeDtypeStruct((rows, columns), f32),
        in_specs=[
            pl.BlockSpec(memory_space=pl.ANY),
            pl.BlockSpec(memory_space=pltpu.VMEM),
            pl.BlockSpec(memory_space=pl.ANY),
            pl.BlockSpec(memory_space=pltpu.VMEM),
        ],
        out_specs=pl.BlockSpec(memory_space=pl.ANY),
        scratch_shapes=[
            pltpu.VMEM((rows, depth), bf16),
            pltpu.VMEM((halves, b_panels.shape[0], HALF), bf16),
            pltpu.VMEM((a_flags.shape[0], depth), f32),
            pltpu.VMEM((b_flags.shape[0], columns), f32),
            taken, taken, taken,
            tile, tile, tile,
            code, code, code, code,
            dma((tiles,)), dma((halves,)), each,
            dma((4, halves)), dma((halves,)), dma((halves,)), dma((halves,)),
            each, each, each, each, each, each,
        ],
        compiler_params=pltpu.CompilerParams(
            collective_id=0, has_side_effects=True, vmem_limit_bytes=60 * 2**20
        ),
        cost_estimate=pl.CostEstimate(
            flops=8 * rows * depth * columns, bytes_accessed=2 * rows * depth + 8 * rows * columns, transcendentals=0
        ),
    )(a_panels, a_flags, b_panels, b_flags)


def solution(mesh):
    placed = (P("row", "col"), P("row", "col"), P("row", "col"), P("row", "col"))
    return jax.shard_map(
        functools.partial(per_device, mesh.shape["row"], mesh.shape["col"]),
        mesh=mesh, in_specs=placed, out_specs=P("row", "col"), check_vma=False,
    )
```

```python
import functools

import jax
import jax.numpy as jnp
from jax import lax
from jax.experimental import pallas as pl
from jax.experimental.pallas import tpu as pltpu
from jax.sharding import PartitionSpec as P

MESH = pl.DeviceIdType.MESH
TILE = 512
GROUP = 256
CHUNK = 128
PAD = 16
FINE = 64.0
PIECES = 4
AHEAD = 2
FIRST, END, SECOND = 1, 2, 3

def lanes_expanded(flags, width, across=1):
    count = flags.shape[across]
    owner = lax.broadcasted_iota(jnp.int32, (count, width), 1) // (width // count)
    spread = (owner == lax.broadcasted_iota(jnp.int32, (count, width), 0)).astype(jnp.float32)
    return lax.dot_general(flags.astype(jnp.float32), spread, (((across,), (0,)), ((), ())), preferred_element_type=jnp.float32)


def coded(value, out_ref):
    for g in range(value.shape[0] // GROUP):
        part = value[g * GROUP : (g + 1) * GROUP]
        largest = jnp.maximum(jnp.max(jnp.abs(part), axis=0, keepdims=True), 1e-30)
        power = jnp.ceil(jnp.log2(largest) * FINE + 0.5)
        scaled = part * (jnp.exp2(power * (-1.0 / FINE)) * 32767.0)
        whole = jnp.round(jnp.clip(scaled, -32767.0, 32767.0))
        start = g * (GROUP + PAD)
        out_ref[pl.ds(start, GROUP), :] = whole.astype(jnp.int32).astype(jnp.int16)
        shown = jnp.broadcast_to(power.astype(jnp.int32), (PAD, part.shape[1]))
        out_ref[pl.ds(start + GROUP, PAD), :] = shown.astype(jnp.int16)


def decoded(in_ref, g):
    start = g * (GROUP + PAD)
    power = in_ref[pl.ds(start + GROUP, PAD), :].astype(jnp.int32).astype(jnp.float32)[0:1, :]
    scale = jnp.exp2(power * (1.0 / FINE)) * (1.0 / 32767.0)
    return in_ref[pl.ds(start, GROUP), :].astype(jnp.int32).astype(jnp.float32) * scale


def kernel(
    n_row, n_col, a_ref, af_ref, b_ref, bf_ref, o_ref,
    left, right, fa, fb, held, relay, spare, kept, acc, xs, xr, qs, qr, zs, zr,
    a_sem, b_sem, own_sem, o_sem, send_r, recv_r,
    send_x, recv_x, send_q, recv_q, send_z, recv_z,
):
    i, j = lax.axis_index("row"), lax.axis_index("col")
    even = lax.rem(j, 2) == 0
    other = jnp.logical_not(even)
    side = lax.rem(j // 2, 2)
    rows, depth = left.shape
    chunks, tiles = held.shape[0], rows // TILE
    part_depth = depth // PIECES

    def at(di, dj):
        return (lax.rem(i + di + n_row, n_row), lax.rem(j + dj + n_col, n_col))

    def either(e, o):
        return tuple(jnp.where(even, p, q) for p, q in zip(e, o, strict=True))

    def load_a(m):
        part = pl.ds(pl.multiple_of(m * TILE, TILE), TILE)
        return pltpu.make_async_copy(a_ref.at[part, :], left.at[part, :], a_sem.at[m])

    def load_b(n):
        return pltpu.make_async_copy(b_ref.at[:, pl.ds(n * CHUNK, CHUNK)], right.at[n], b_sem.at[n])

    load_b(0).start()

    barrier = pltpu.get_barrier_semaphore()
    near = [(-2, 4 * side), (2, -4 * side), (-2, 0), (2, 0), (4, 0), (-1, 3), (-1, -1), (1, -3), (1, 1), (1, -1), (-1, 1)]
    near += [(0, d) for d in (-3, -2, -1, 1, 2, 3)]
    for di, dj in near:
        pl.semaphore_signal(barrier, inc=1, device_id=at(di, dj), device_id_type=MESH)

    fb[...] = lanes_expanded(bf_ref[...], fb.shape[1], 0)
    size_b = b_ref.shape[0] // fb.shape[0]

    def mask_b(n):
        @pl.loop(0, fb.shape[0] // 8)
        def _(k):
            flags = fb[pl.ds(pl.multiple_of(k * 8, 8), 8), pl.ds(n * CHUNK, CHUNK)]
            for r in range(8):
                part = pl.ds(pl.multiple_of((k * 8 + r) * size_b, size_b), size_b)
                right[n, part, :] = right[n, part, :] * flags[r : r + 1].astype(jnp.bfloat16)

    own = lax.rem(i + j, n_col) // n_row

    def half_for(s):
        return lax.rem(own + jnp.where(i < s, 1, 0), 2)

    def block(n, half):
        return right.at[n, pl.ds(pl.multiple_of(half * depth, depth), depth), :]

    def piece(n, u, half):
        start = pl.multiple_of(half * depth + u * part_depth, part_depth)
        return right.at[n, pl.ds(start, part_depth), :]

    def place(n, u, slot):
        return held.at[n, pl.ds(u * part_depth, part_depth), pl.ds(slot * CHUNK, CHUNK)]

    def passing(n, u):
        return relay.at[n, pl.ds(u * part_depth, part_depth), :]

    def passing_too(n, u):
        return spare.at[n, pl.ds(u * part_depth, part_depth), :]

    def remote(src, dst, ssem, rsem, where):
        return pltpu.make_async_remote_copy(
            src_ref=src, dst_ref=dst, send_sem=ssem, recv_sem=rsem, device_id=where, device_id_type=MESH
        )

    OWN, Z, X, Y, VIA, TOO, EXTRA = range(7)

    def send_via(n, u):
        return remote(
            piece(n, u, half_for(2)), passing(n, u), send_r.at[VIA, n, u], recv_r.at[VIA, n, u], at(-2, 4 * side)
        )

    def hand_y(n, u):
        return remote(
            passing(n, u), place(n, u, Y), send_r.at[Y, n, u], recv_r.at[Y, n, u], at(0, 2 - 4 * side)
        )

    def hand_x(n, u):
        to = either(at(-1, 3 - 4 * side), at(1, 1 - 4 * side))
        return remote(passing(n, u), place(n, u, X), send_r.at[X, n, u], recv_r.at[X, n, u], to)

    def hand_z(n, u):
        to = either(at(1, -1), at(-1, 1))
        return remote(place(n, u, Y), place(n, u, Z), send_r.at[Z, n, u], recv_r.at[Z, n, u], to)

    def send_too(n, u):
        first = i == 1
        half = jnp.where(first, half_for(1), half_for(3))
        across = jnp.where(even, 4 * side, 0)
        to = tuple(jnp.where(first, p, q) for p, q in zip(at(4, 0), at(-2, across), strict=True))
        return remote(piece(n, u, half), passing_too(n, u), send_r.at[TOO, n, u], recv_r.at[TOO, n, u], to)

    def pass_too(n, u):
        return remote(passing_too(n, u), passing_too(n, u), send_r.at[EXTRA, n, u], recv_r.at[TOO, n, u], at(2, 0))

    def hand_too(n, u, slot):
        first = i == n_row - 1
        back = at(-1, 3 - jnp.where(even, 4 * side, 0))
        to = tuple(jnp.where(first, p, q) for p, q in zip(at(1, 1), back, strict=True))
        return remote(passing_too(n, u), place(n, u, slot), send_r.at[EXTRA, n, u], recv_r.at[slot, n, u], to)

    gives_x = jnp.where(even, i != 0, i != n_row - 1)
    gives_z = jnp.where(even, i != n_row - 1, i != 0)
    sends_too = jnp.logical_or(i == 1, i == 2)
    passes_too = jnp.logical_or(i == 5, jnp.logical_or(i == 0, i == n_row - 1))

    def begin(n, u):
        send_via(n, u).start()

        @pl.when(sends_too)
        def _():
            send_too(n, u).start()

    def hand_on(n, u):
        send_via(n, u).wait_recv()
        hand_y(n, u).start()

        @pl.when(gives_x)
        def _():
            hand_x(n, u).start()

        @pl.when(i == 5)
        def _():
            send_too(n, u).wait_recv()
            pass_too(n, u).start()

        @pl.when(i == 0)
        def _():
            send_too(n, u).wait_recv()

        @pl.when(jnp.logical_and(even, i == 0))
        def _():
            hand_too(n, u, X).start()

        @pl.when(jnp.logical_and(other, i == 0))
        def _():
            hand_too(n, u, Z).start()

    def hand_third(n, u):
        hand_y(n, u).wait_recv()

        @pl.when(gives_z)
        def _():
            hand_z(n, u).start()

        @pl.when(i == n_row - 1)
        def _():
            send_too(n, u).wait_recv()

        @pl.when(jnp.logical_and(even, i == n_row - 1))
        def _():
            hand_too(n, u, Z).start()

        @pl.when(jnp.logical_and(other, i == n_row - 1))
        def _():
            hand_too(n, u, X).start()

    def own_copy(n):
        return pltpu.make_async_copy(block(n, own), held.at[n, :, pl.ds(0, CHUNK)], own_sem.at[n])

    load_b(0).wait()
    for n in range(1, chunks):
        load_b(n).start()
    for m in range(tiles):
        load_a(m).start()
    mask_b(0)
    pl.semaphore_wait(barrier, len(near))
    for u in range(AHEAD):
        begin(0, u)
    own_copy(0).start()
    for n in range(1, chunks):
        load_b(n).wait()
        mask_b(n)
        own_copy(n).start()

    fa[...] = lanes_expanded(af_ref[...], depth)
    size_a = rows // fa.shape[0]

    @pl.loop(0, tiles)
    def _(m):
        load_a(m).wait()

        @pl.loop(0, TILE // size_a)
        def _(k):
            part = pl.ds(pl.multiple_of(m * TILE + k * size_a, size_a), size_a)
            row = fa[pl.ds(m * (TILE // size_a) + k, 1), :].astype(jnp.bfloat16)
            left[part, :] = left[part, :] * row

    for n in range(chunks):
        own_copy(n).wait()

    partner = either(at(0, 1), at(0, -1))

    def x_copy(n, m):
        return remote(xs.at[n, m], xr.at[n, m], send_x.at[n, m], recv_x.at[n, m], partner)

    def q_copy(n, m):
        return remote(qs.at[n, m], qr.at[n, m], send_q.at[n, m], recv_q.at[n, m], at(0, -2))

    def z_copy(n, m):
        return remote(zs.at[n, m], zr.at[n, m], send_z.at[n, m], recv_z.at[n, m], either(at(0, -3), at(0, -1)))

    def product(n, m, first):
        part = pl.ds(pl.multiple_of(m * TILE, TILE), TILE)
        pair = held[n, :, first * CHUNK : (first + 2) * CHUNK]
        return jnp.dot(left[part, :], pair, preferred_element_type=jnp.float32)

    def first_pair(n):
        for u in range(PIECES):
            hand_x(n, u).wait_recv()

        @pl.loop(0, tiles)
        def _(m):
            value = product(n, m, X)
            xs[n, m] = value[:, :CHUNK]
            x_copy(n, m).start()
            kept[m] = value[:, CHUNK:]

    def first_end(n):
        @pl.loop(0, tiles)
        def _(m):
            x_copy(n, m).wait_recv()
            coded(kept[m] + xr[n, m], qs.at[n, m])
            q_copy(n, m).start()

    def second_pair(n):
        for u in range(PIECES):
            hand_z(n, u).wait_recv()

        @pl.loop(0, tiles)
        def _(m):
            value = product(n, m, OWN)
            acc[n, m] = value[:, :CHUNK]
            coded(value[:, CHUNK:], zs.at[n, m])
            z_copy(n, m).start()

    @pl.loop(0, chunks)
    def _(n):
        for u in range(PIECES):
            ahead, rest = divmod(u + AHEAD, PIECES)

            @pl.when(n + ahead < chunks)
            def _():
                begin(n + ahead, rest)

            hand_on(n, u)
            if u == 0:
                @pl.when(n > 0)
                def _():
                    hand_third(n - 1, PIECES - 1)
            else:
                hand_third(n, u - 1)
            if u == FIRST:
                @pl.when(n > 0)
                def _():
                    first_pair(n - 1)
            if u == END:
                @pl.when(n > 0)
                def _():
                    first_end(n - 1)
            if u == SECOND:
                @pl.when(n > 0)
                def _():
                    second_pair(n - 1)

    hand_third(chunks - 1, PIECES - 1)
    first_pair(chunks - 1)
    first_end(chunks - 1)
    second_pair(chunks - 1)

    def store(n, m):
        where = o_ref.at[
            pl.ds(pl.multiple_of(m * TILE, TILE), TILE), pl.ds(pl.multiple_of(n * CHUNK, CHUNK), CHUNK)
        ]
        return pltpu.make_async_copy(acc.at[n, m], where, o_sem.at[n, m])

    @pl.loop(0, chunks)
    def _(n):
        @pl.loop(0, tiles)
        def _(m):
            q_copy(n, m).wait_recv()
            z_copy(n, m).wait_recv()
            for g in range(TILE // GROUP):
                part = pl.ds(g * GROUP, GROUP)
                acc[n, m, part, :] = acc[n, m, part, :] + decoded(qr.at[n, m], g) + decoded(zr.at[n, m], g)
            store(n, m).start()

    @pl.loop(0, chunks)
    def _(n):
        for u in range(PIECES):
            send_via(n, u).wait_send()
            hand_y(n, u).wait_send()

            @pl.when(gives_x)
            def _():
                hand_x(n, u).wait_send()

            @pl.when(gives_z)
            def _():
                hand_z(n, u).wait_send()

            @pl.when(sends_too)
            def _():
                send_too(n, u).wait_send()

            @pl.when(passes_too)
            def _():
                pass_too(n, u).wait_send()

        @pl.loop(0, tiles)
        def _(m):
            x_copy(n, m).wait_send()
            q_copy(n, m).wait_send()
            z_copy(n, m).wait_send()
            store(n, m).wait()


def per_device(n_row, n_col, a_panels, a_flags, b_panels, b_flags):
    rows, depth = a_panels.shape
    columns = b_panels.shape[1]
    chunks, tiles = columns // CHUNK, rows // TILE
    bf16, f32, dma = jnp.bfloat16, jnp.float32, pltpu.SemaphoreType.DMA
    tile = pltpu.VMEM((chunks, tiles, TILE, CHUNK), f32)
    code = pltpu.VMEM((chunks, tiles, TILE // GROUP * (GROUP + PAD), CHUNK), jnp.int16)
    each = dma((chunks, tiles))
    return pl.pallas_call(
        functools.partial(kernel, n_row, n_col),
        name="block_products",
        out_shape=jax.ShapeDtypeStruct((rows, columns), f32),
        in_specs=[
            pl.BlockSpec(memory_space=pl.ANY),
            pl.BlockSpec(memory_space=pltpu.VMEM),
            pl.BlockSpec(memory_space=pl.ANY),
            pl.BlockSpec(memory_space=pltpu.VMEM),
        ],
        out_specs=pl.BlockSpec(memory_space=pl.ANY),
        scratch_shapes=[
            pltpu.VMEM((rows, depth), bf16),
            pltpu.VMEM((chunks, b_panels.shape[0], CHUNK), bf16),
            pltpu.VMEM((a_flags.shape[0], depth), f32),
            pltpu.VMEM((b_flags.shape[0], columns), f32),
            pltpu.VMEM((chunks, depth, 4 * CHUNK), bf16),
            pltpu.VMEM((chunks, depth, CHUNK), bf16),
            pltpu.VMEM((chunks, depth, CHUNK), bf16),
            pltpu.VMEM((tiles, TILE, CHUNK), f32),
            tile, tile, tile,
            code, code, code, code,
            dma((tiles,)), dma((chunks,)), dma((chunks,)), each,
            dma((7, chunks, PIECES)), dma((6, chunks, PIECES)),
            each, each, each, each, each, each,
        ],
        compiler_params=pltpu.CompilerParams(
            collective_id=0, has_side_effects=True, vmem_limit_bytes=60 * 2**20
        ),
        cost_estimate=pl.CostEstimate(
            flops=8 * rows * depth * columns, bytes_accessed=2 * rows * depth + 8 * rows * columns, transcendentals=0
        ),
    )(a_panels, a_flags, b_panels, b_flags.T)


def solution(mesh):
    placed = (P("row", "col"), P("row", "col"), P("row", "col"), P("row", "col"))
    return jax.shard_map(
        functools.partial(per_device, mesh.shape["row"], mesh.shape["col"]),
        mesh=mesh, in_specs=placed, out_specs=P("row", "col"), check_vma=False,
    )
```

```python
import functools

import jax
import jax.numpy as jnp
from jax import lax
from jax.experimental import pallas as pl
from jax.experimental.pallas import tpu as pltpu
from jax.sharding import PartitionSpec as P

MESH = pl.DeviceIdType.MESH
TILE = 512
GROUP = 256
CHUNK = 128
PAD = 16
FINE = 64.0
PIECES = 4
AHEAD = 2
LEAD = 3
FIRST, END, SECOND = 1, 2, 3

def lanes_expanded(flags, width, across=1):
    count = flags.shape[across]
    owner = lax.broadcasted_iota(jnp.int32, (count, width), 1) // (width // count)
    spread = (owner == lax.broadcasted_iota(jnp.int32, (count, width), 0)).astype(jnp.float32)
    return lax.dot_general(flags.astype(jnp.float32), spread, (((across,), (0,)), ((), ())), preferred_element_type=jnp.float32)


def coded(value, out_ref):
    for g in range(value.shape[0] // GROUP):
        part = value[g * GROUP : (g + 1) * GROUP]
        largest = jnp.maximum(jnp.max(jnp.abs(part), axis=0, keepdims=True), 1e-30)
        power = jnp.ceil(jnp.log2(largest) * FINE + 0.5)
        scaled = part * (jnp.exp2(power * (-1.0 / FINE)) * 32767.0)
        whole = jnp.round(jnp.clip(scaled, -32767.0, 32767.0))
        start = g * (GROUP + PAD)
        out_ref[pl.ds(start, GROUP), :] = whole.astype(jnp.int32).astype(jnp.int16)
        shown = jnp.broadcast_to(power.astype(jnp.int32), (PAD, part.shape[1]))
        out_ref[pl.ds(start + GROUP, PAD), :] = shown.astype(jnp.int16)


def decoded(in_ref, g):
    start = g * (GROUP + PAD)
    power = in_ref[pl.ds(start + GROUP, PAD), :].astype(jnp.int32).astype(jnp.float32)[0:1, :]
    scale = jnp.exp2(power * (1.0 / FINE)) * (1.0 / 32767.0)
    return in_ref[pl.ds(start, GROUP), :].astype(jnp.int32).astype(jnp.float32) * scale


def kernel(
    n_row, n_col, a_ref, af_ref, b_ref, bf_ref, o_ref,
    left, right, fa, fb, held, relay, spare, kept, acc, xs, xr, qs, qr, zs, zr,
    a_sem, b_sem, own_sem, o_sem, send_r, recv_r,
    send_x, recv_x, send_q, recv_q, send_z, recv_z,
):
    i, j = lax.axis_index("row"), lax.axis_index("col")
    even = lax.rem(j, 2) == 0
    other = jnp.logical_not(even)
    side = lax.rem(j // 2, 2)
    rows, depth = left.shape
    chunks, tiles = held.shape[0], rows // TILE
    part_depth = depth // PIECES

    def at(di, dj):
        return (lax.rem(i + di + n_row, n_row), lax.rem(j + dj + n_col, n_col))

    def either(e, o):
        return tuple(jnp.where(even, p, q) for p, q in zip(e, o, strict=True))

    def load_a(m):
        part = pl.ds(pl.multiple_of(m * TILE, TILE), TILE)
        return pltpu.make_async_copy(a_ref.at[part, :], left.at[part, :], a_sem.at[m])

    def load_b(n):
        return pltpu.make_async_copy(b_ref.at[:, pl.ds(n * CHUNK, CHUNK)], right.at[n], b_sem.at[n])

    load_b(0).start()

    barrier = pltpu.get_barrier_semaphore()
    near = [(-2, 4 * side), (2, -4 * side), (-2, 0), (2, 0), (4, 0), (-1, 3), (-1, -1), (1, -3), (1, 1), (1, -1), (-1, 1)]
    near += [(4, 2 - 4 * side), (2, 2 - 4 * side), (-2, 2 - 4 * side), (1, 3), (-1, -3), (-1, 5), (1, -5)]
    near += [(0, d) for d in (-3, -2, -1, 1, 2, 3)]
    for di, dj in near:
        pl.semaphore_signal(barrier, inc=1, device_id=at(di, dj), device_id_type=MESH)

    fb[...] = lanes_expanded(bf_ref[...], fb.shape[1], 0)
    size_b = b_ref.shape[0] // fb.shape[0]

    def mask_b(n):
        @pl.loop(0, fb.shape[0] // 8)
        def _(k):
            flags = fb[pl.ds(pl.multiple_of(k * 8, 8), 8), pl.ds(n * CHUNK, CHUNK)]
            for r in range(8):
                part = pl.ds(pl.multiple_of((k * 8 + r) * size_b, size_b), size_b)
                right[n, part, :] = right[n, part, :] * flags[r : r + 1].astype(jnp.bfloat16)

    own = lax.rem(i + j, n_col) // n_row

    def half_for(s):
        return lax.rem(own + jnp.where(i < s, 1, 0), 2)

    def block(n, half):
        return right.at[n, pl.ds(pl.multiple_of(half * depth, depth), depth), :]

    def piece(n, u, half):
        start = pl.multiple_of(half * depth + u * part_depth, part_depth)
        return right.at[n, pl.ds(start, part_depth), :]

    def place(n, u, slot):
        return held.at[n, pl.ds(u * part_depth, part_depth), pl.ds(slot * CHUNK, CHUNK)]

    def passing(n, u):
        return relay.at[n, pl.ds(u * part_depth, part_depth), :]

    def passing_too(n, u):
        return spare.at[n, pl.ds(u * part_depth, part_depth), :]

    def remote(src, dst, ssem, rsem, where):
        return pltpu.make_async_remote_copy(
            src_ref=src, dst_ref=dst, send_sem=ssem, recv_sem=rsem, device_id=where, device_id_type=MESH
        )

    OWN, Z, X, Y, VIA, TOO, EXTRA = range(7)

    def send_via(n, u):
        return remote(
            piece(n, u, half_for(2)), passing(n, u), send_r.at[VIA, n, u], recv_r.at[VIA, n, u], at(-2, 4 * side)
        )

    def hand_y(n, u):
        return remote(
            passing(n, u), place(n, u, Y), send_r.at[Y, n, u], recv_r.at[Y, n, u], at(0, 2 - 4 * side)
        )

    def hand_x(n, u):
        to = either(at(-1, 3 - 4 * side), at(1, 1 - 4 * side))
        return remote(passing(n, u), place(n, u, X), send_r.at[X, n, u], recv_r.at[X, n, u], to)

    def hand_z(n, u):
        to = either(at(1, -1), at(-1, 1))
        return remote(place(n, u, Y), place(n, u, Z), send_r.at[Z, n, u], recv_r.at[Z, n, u], to)

    def aside(u):
        return 2 - 4 * side if u % 2 else 0

    def send_too(n, u):
        first = i == 1
        half = jnp.where(first, half_for(1), half_for(3))
        across = jnp.where(even, 4 * side, aside(u))
        to = tuple(jnp.where(first, p, q) for p, q in zip(at(4, jnp.where(even, aside(u), 0)), at(-2, across), strict=True))
        return remote(piece(n, u, half), passing_too(n, u), send_r.at[TOO, n, u], recv_r.at[TOO, n, u], to)

    def pass_too(n, u):
        return remote(passing_too(n, u), passing_too(n, u), send_r.at[EXTRA, n, u], recv_r.at[TOO, n, u], at(2, 0))

    def hand_too(n, u, slot):
        first = i == n_row - 1
        back = at(-1, 3 + jnp.where(even, -4 * side, aside(u)))
        to = tuple(jnp.where(first, p, q) for p, q in zip(at(1, 1 + jnp.where(even, aside(u), 0)), back, strict=True))
        return remote(passing_too(n, u), place(n, u, slot), send_r.at[EXTRA, n, u], recv_r.at[slot, n, u], to)

    gives_x = jnp.where(even, i != 0, i != n_row - 1)
    gives_z = jnp.where(even, i != n_row - 1, i != 0)
    sends_too = jnp.logical_or(i == 1, i == 2)
    passes_too = jnp.logical_or(i == 5, jnp.logical_or(i == 0, i == n_row - 1))

    def begin(n, u):
        send_via(n, u).start()

        @pl.when(i == 2)
        def _():
            send_too(n, u).start()

    def begin_too(n, u):
        @pl.when(i == 1)
        def _():
            send_too(n, u).start()

    def go_on_too(n, u):
        @pl.when(i == 5)
        def _():
            send_too(n, u).wait_recv()
            pass_too(n, u).start()

    def hand_on(n, u):
        send_via(n, u).wait_recv()
        hand_y(n, u).start()

        @pl.when(gives_x)
        def _():
            hand_x(n, u).start()

        @pl.when(jnp.logical_or(i == 0, i == n_row - 1))
        def _():
            send_too(n, u).wait_recv()

        @pl.when(jnp.where(even, i == 0, i == n_row - 1))
        def _():
            hand_too(n, u, X).start()

        @pl.when(jnp.where(even, i == n_row - 1, i == 0))
        def _():
            hand_too(n, u, Z).start()

    def hand_third(n, u):
        hand_y(n, u).wait_recv()

        @pl.when(gives_z)
        def _():
            hand_z(n, u).start()

    def own_copy(n):
        return pltpu.make_async_copy(block(n, own), held.at[n, :, pl.ds(0, CHUNK)], own_sem.at[n])

    load_b(0).wait()
    for n in range(1, chunks):
        load_b(n).start()
    for m in range(tiles):
        load_a(m).start()
    mask_b(0)
    pl.semaphore_wait(barrier, len(near))
    for u in range(AHEAD):
        begin(0, u)
    for u in range(min(AHEAD + LEAD, PIECES)):
        begin_too(0, u)
    own_copy(0).start()
    for n in range(1, chunks):
        load_b(n).wait()
        mask_b(n)
        own_copy(n).start()
        for u in range(min(AHEAD + LEAD - n * PIECES, PIECES)):
            begin_too(n, u)

    fa[...] = lanes_expanded(af_ref[...], depth)
    size_a = rows // fa.shape[0]

    @pl.loop(0, tiles)
    def _(m):
        load_a(m).wait()

        @pl.loop(0, TILE // size_a)
        def _(k):
            part = pl.ds(pl.multiple_of(m * TILE + k * size_a, size_a), size_a)
            row = fa[pl.ds(m * (TILE // size_a) + k, 1), :].astype(jnp.bfloat16)
            left[part, :] = left[part, :] * row

    for n in range(chunks):
        own_copy(n).wait()

    partner = either(at(0, 1), at(0, -1))

    def x_copy(n, m):
        return remote(xs.at[n, m], xr.at[n, m], send_x.at[n, m], recv_x.at[n, m], partner)

    def q_copy(n, m):
        return remote(qs.at[n, m], qr.at[n, m], send_q.at[n, m], recv_q.at[n, m], at(0, -2))

    def z_copy(n, m):
        return remote(zs.at[n, m], zr.at[n, m], send_z.at[n, m], recv_z.at[n, m], either(at(0, -3), at(0, -1)))

    for u in range(LEAD):
        go_on_too(u // PIECES, u % PIECES)

    def product(n, m, first):
        part = pl.ds(pl.multiple_of(m * TILE, TILE), TILE)
        pair = held[n, :, first * CHUNK : (first + 2) * CHUNK]
        return jnp.dot(left[part, :], pair, preferred_element_type=jnp.float32)

    def first_pair(n):
        for u in range(PIECES):
            hand_x(n, u).wait_recv()

        @pl.loop(0, tiles)
        def _(m):
            value = product(n, m, X)
            xs[n, m] = value[:, :CHUNK]
            x_copy(n, m).start()
            kept[m] = value[:, CHUNK:]

    def first_end(n):
        @pl.loop(0, tiles)
        def _(m):
            x_copy(n, m).wait_recv()
            coded(kept[m] + xr[n, m], qs.at[n, m])
            q_copy(n, m).start()

    def second_pair(n):
        for u in range(PIECES):
            hand_z(n, u).wait_recv()

        @pl.loop(0, tiles)
        def _(m):
            value = product(n, m, OWN)
            acc[n, m] = value[:, :CHUNK]
            coded(value[:, CHUNK:], zs.at[n, m])
            z_copy(n, m).start()

    @pl.loop(0, chunks)
    def _(n):
        for u in range(PIECES):
            ahead, rest = divmod(u + AHEAD, PIECES)

            @pl.when(n + ahead < chunks)
            def _():
                begin(n + ahead, rest)

            later, rest_later = divmod(u + AHEAD + LEAD, PIECES)

            @pl.when(n + later < chunks)
            def _():
                begin_too(n + later, rest_later)

            soon, rest_soon = divmod(u + LEAD, PIECES)

            @pl.when(n + soon < chunks)
            def _():
                go_on_too(n + soon, rest_soon)

            hand_on(n, u)
            if u == 0:
                @pl.when(n > 0)
                def _():
                    hand_third(n - 1, PIECES - 1)
            else:
                hand_third(n, u - 1)
            if u == FIRST:
                @pl.when(n > 0)
                def _():
                    first_pair(n - 1)
            if u == END:
                @pl.when(n > 0)
                def _():
                    first_end(n - 1)
            if u == SECOND:
                @pl.when(n > 0)
                def _():
                    second_pair(n - 1)

    hand_third(chunks - 1, PIECES - 1)
    first_pair(chunks - 1)
    first_end(chunks - 1)
    second_pair(chunks - 1)

    def store(n, m):
        where = o_ref.at[
            pl.ds(pl.multiple_of(m * TILE, TILE), TILE), pl.ds(pl.multiple_of(n * CHUNK, CHUNK), CHUNK)
        ]
        return pltpu.make_async_copy(acc.at[n, m], where, o_sem.at[n, m])

    @pl.loop(0, chunks)
    def _(n):
        @pl.loop(0, tiles)
        def _(m):
            q_copy(n, m).wait_recv()
            z_copy(n, m).wait_recv()
            for g in range(TILE // GROUP):
                part = pl.ds(g * GROUP, GROUP)
                acc[n, m, part, :] = acc[n, m, part, :] + decoded(qr.at[n, m], g) + decoded(zr.at[n, m], g)
            store(n, m).start()

    @pl.loop(0, chunks)
    def _(n):
        for u in range(PIECES):
            send_via(n, u).wait_send()
            hand_y(n, u).wait_send()

            @pl.when(gives_x)
            def _():
                hand_x(n, u).wait_send()

            @pl.when(gives_z)
            def _():
                hand_z(n, u).wait_send()

            @pl.when(sends_too)
            def _():
                send_too(n, u).wait_send()

            @pl.when(passes_too)
            def _():
                pass_too(n, u).wait_send()

        @pl.loop(0, tiles)
        def _(m):
            x_copy(n, m).wait_send()
            q_copy(n, m).wait_send()
            z_copy(n, m).wait_send()
            store(n, m).wait()


def per_device(n_row, n_col, a_panels, a_flags, b_panels, b_flags):
    rows, depth = a_panels.shape
    columns = b_panels.shape[1]
    chunks, tiles = columns // CHUNK, rows // TILE
    bf16, f32, dma = jnp.bfloat16, jnp.float32, pltpu.SemaphoreType.DMA
    tile = pltpu.VMEM((chunks, tiles, TILE, CHUNK), f32)
    code = pltpu.VMEM((chunks, tiles, TILE // GROUP * (GROUP + PAD), CHUNK), jnp.int16)
    each = dma((chunks, tiles))
    return pl.pallas_call(
        functools.partial(kernel, n_row, n_col),
        name="block_products",
        out_shape=jax.ShapeDtypeStruct((rows, columns), f32),
        in_specs=[
            pl.BlockSpec(memory_space=pl.ANY),
            pl.BlockSpec(memory_space=pltpu.VMEM),
            pl.BlockSpec(memory_space=pl.ANY),
            pl.BlockSpec(memory_space=pltpu.VMEM),
        ],
        out_specs=pl.BlockSpec(memory_space=pl.ANY),
        scratch_shapes=[
            pltpu.VMEM((rows, depth), bf16),
            pltpu.VMEM((chunks, b_panels.shape[0], CHUNK), bf16),
            pltpu.VMEM((a_flags.shape[0], depth), f32),
            pltpu.VMEM((b_flags.shape[0], columns), f32),
            pltpu.VMEM((chunks, depth, 4 * CHUNK), bf16),
            pltpu.VMEM((chunks, depth, CHUNK), bf16),
            pltpu.VMEM((chunks, depth, CHUNK), bf16),
            pltpu.VMEM((tiles, TILE, CHUNK), f32),
            tile, tile, tile,
            code, code, code, code,
            dma((tiles,)), dma((chunks,)), dma((chunks,)), each,
            dma((7, chunks, PIECES)), dma((6, chunks, PIECES)),
            each, each, each, each, each, each,
        ],
        compiler_params=pltpu.CompilerParams(
            collective_id=0, has_side_effects=True, vmem_limit_bytes=60 * 2**20
        ),
        cost_estimate=pl.CostEstimate(
            flops=8 * rows * depth * columns, bytes_accessed=2 * rows * depth + 8 * rows * columns, transcendentals=0
        ),
    )(a_panels, a_flags, b_panels, b_flags.T)


def solution(mesh):
    placed = (P("row", "col"), P("row", "col"), P("row", "col"), P("row", "col"))
    return jax.shard_map(
        functools.partial(per_device, mesh.shape["row"], mesh.shape["col"]),
        mesh=mesh, in_specs=placed, out_specs=P("row", "col"), check_vma=False,
    )
```

```python
import functools

import jax
import jax.numpy as jnp
from jax import lax
from jax.experimental import pallas as pl
from jax.experimental.pallas import tpu as pltpu
from jax.sharding import PartitionSpec as P

MESH = pl.DeviceIdType.MESH
TILE = 512
GROUP = 256
CHUNK = 128
PAD = 16
FINE = 64.0
PIECES = 4
AHEAD = 2
LEAD = 3

def lanes_expanded(flags, width, across=1):
    count = flags.shape[across]
    owner = lax.broadcasted_iota(jnp.int32, (count, width), 1) // (width // count)
    spread = (owner == lax.broadcasted_iota(jnp.int32, (count, width), 0)).astype(jnp.float32)
    return lax.dot_general(flags.astype(jnp.float32), spread, (((across,), (0,)), ((), ())), preferred_element_type=jnp.float32)


def coded(value, out_ref):
    for g in range(value.shape[0] // GROUP):
        part = value[g * GROUP : (g + 1) * GROUP]
        largest = jnp.maximum(jnp.max(jnp.abs(part), axis=0, keepdims=True), 1e-30)
        power = jnp.ceil(jnp.log2(largest) * FINE + 0.5)
        scaled = part * (jnp.exp2(power * (-1.0 / FINE)) * 32767.0)
        whole = jnp.round(jnp.clip(scaled, -32767.0, 32767.0))
        start = g * (GROUP + PAD)
        out_ref[pl.ds(start, GROUP), :] = whole.astype(jnp.int32).astype(jnp.int16)
        shown = jnp.broadcast_to(power.astype(jnp.int32), (PAD, part.shape[1]))
        out_ref[pl.ds(start + GROUP, PAD), :] = shown.astype(jnp.int16)


def decoded(in_ref, g):
    start = g * (GROUP + PAD)
    power = in_ref[pl.ds(start + GROUP, PAD), :].astype(jnp.int32).astype(jnp.float32)[0:1, :]
    scale = jnp.exp2(power * (1.0 / FINE)) * (1.0 / 32767.0)
    return in_ref[pl.ds(start, GROUP), :].astype(jnp.int32).astype(jnp.float32) * scale


def kernel(
    n_row, n_col, a_ref, af_ref, b_ref, bf_ref, o_ref,
    left, right, fa, fb, held, relay, spare, kept, acc, xs, xr, qs, qr, zs, zr,
    a_sem, b_sem, own_sem, o_sem, send_r, recv_r,
    send_x, recv_x, send_q, recv_q, send_z, recv_z,
):
    i, j = lax.axis_index("row"), lax.axis_index("col")
    even = lax.rem(j, 2) == 0
    other = jnp.logical_not(even)
    side = lax.rem(j // 2, 2)
    rows, depth = left.shape
    chunks, tiles = held.shape[0], rows // TILE
    part_depth = depth // PIECES

    def at(di, dj):
        return (lax.rem(i + di + n_row, n_row), lax.rem(j + dj + n_col, n_col))

    def either(e, o):
        return tuple(jnp.where(even, p, q) for p, q in zip(e, o, strict=True))

    def load_a(m):
        part = pl.ds(pl.multiple_of(m * TILE, TILE), TILE)
        return pltpu.make_async_copy(a_ref.at[part, :], left.at[part, :], a_sem.at[m])

    def load_b(n):
        return pltpu.make_async_copy(b_ref.at[:, pl.ds(n * CHUNK, CHUNK)], right.at[n], b_sem.at[n])

    load_b(0).start()

    barrier = pltpu.get_barrier_semaphore()
    near = [(-2, 4 * side), (2, -4 * side), (-2, 0), (2, 0), (4, 0), (-1, 3), (-1, -1), (1, -3), (1, 1), (1, -1), (-1, 1)]
    near += [(4, 2 - 4 * side), (2, 2 - 4 * side), (-2, 2 - 4 * side), (1, 3), (-1, -3), (-1, 5), (1, -5)]
    near += [(0, d) for d in (-3, -2, -1, 1, 2, 3)]
    for di, dj in near:
        pl.semaphore_signal(barrier, inc=1, device_id=at(di, dj), device_id_type=MESH)

    fb[...] = lanes_expanded(bf_ref[...], fb.shape[1], 0)
    size_b = b_ref.shape[0] // fb.shape[0]

    def mask_b(n):
        @pl.loop(0, fb.shape[0] // 8)
        def _(k):
            flags = fb[pl.ds(pl.multiple_of(k * 8, 8), 8), pl.ds(n * CHUNK, CHUNK)]
            for r in range(8):
                part = pl.ds(pl.multiple_of((k * 8 + r) * size_b, size_b), size_b)
                right[n, part, :] = right[n, part, :] * flags[r : r + 1].astype(jnp.bfloat16)

    own = lax.rem(i + j, n_col) // n_row

    def half_for(s):
        return lax.rem(own + jnp.where(i < s, 1, 0), 2)

    def block(n, half):
        return right.at[n, pl.ds(pl.multiple_of(half * depth, depth), depth), :]

    def piece(n, u, half):
        start = pl.multiple_of(half * depth + u * part_depth, part_depth)
        return right.at[n, pl.ds(start, part_depth), :]

    def place(n, u, slot):
        return held.at[n, pl.ds(u * part_depth, part_depth), pl.ds(slot * CHUNK, CHUNK)]

    def passing(n, u):
        return relay.at[n, pl.ds(u * part_depth, part_depth), :]

    def passing_too(n, u):
        return spare.at[n, pl.ds(u * part_depth, part_depth), :]

    def remote(src, dst, ssem, rsem, where):
        return pltpu.make_async_remote_copy(
            src_ref=src, dst_ref=dst, send_sem=ssem, recv_sem=rsem, device_id=where, device_id_type=MESH
        )

    OWN, Z, X, Y, VIA, TOO, EXTRA = range(7)

    def send_via(n, u):
        return remote(
            piece(n, u, half_for(2)), passing(n, u), send_r.at[VIA, n, u], recv_r.at[VIA, n, u], at(-2, 4 * side)
        )

    def hand_y(n, u):
        return remote(
            passing(n, u), place(n, u, Y), send_r.at[Y, n, u], recv_r.at[Y, n, u], at(0, 2 - 4 * side)
        )

    def hand_x(n, u):
        to = either(at(-1, 3 - 4 * side), at(1, 1 - 4 * side))
        return remote(passing(n, u), place(n, u, X), send_r.at[X, n, u], recv_r.at[X, n, u], to)

    def hand_z(n, u):
        to = either(at(1, -1), at(-1, 1))
        return remote(place(n, u, Y), place(n, u, Z), send_r.at[Z, n, u], recv_r.at[Z, n, u], to)

    def aside(u):
        return 2 - 4 * side if u % 2 else 0

    def send_too(n, u):
        first = i == 1
        half = jnp.where(first, half_for(1), half_for(3))
        across = jnp.where(even, 4 * side, aside(u))
        to = tuple(jnp.where(first, p, q) for p, q in zip(at(4, jnp.where(even, aside(u), 0)), at(-2, across), strict=True))
        return remote(piece(n, u, half), passing_too(n, u), send_r.at[TOO, n, u], recv_r.at[TOO, n, u], to)

    def pass_too(n, u):
        return remote(passing_too(n, u), passing_too(n, u), send_r.at[EXTRA, n, u], recv_r.at[TOO, n, u], at(2, 0))

    def hand_too(n, u, slot):
        first = i == n_row - 1
        back = at(-1, 3 + jnp.where(even, -4 * side, aside(u)))
        to = tuple(jnp.where(first, p, q) for p, q in zip(at(1, 1 + jnp.where(even, aside(u), 0)), back, strict=True))
        return remote(passing_too(n, u), place(n, u, slot), send_r.at[EXTRA, n, u], recv_r.at[slot, n, u], to)

    gives_x = jnp.where(even, i != 0, i != n_row - 1)
    gives_z = jnp.where(even, i != n_row - 1, i != 0)
    sends_too = jnp.logical_or(i == 1, i == 2)
    passes_too = jnp.logical_or(i == 5, jnp.logical_or(i == 0, i == n_row - 1))

    def begin(n, u):
        send_via(n, u).start()

        @pl.when(i == 2)
        def _():
            send_too(n, u).start()

    def begin_too(n, u):
        @pl.when(i == 1)
        def _():
            send_too(n, u).start()

    def go_on_too(n, u):
        @pl.when(i == 5)
        def _():
            send_too(n, u).wait_recv()
            pass_too(n, u).start()

    def hand_on(n, u):
        send_via(n, u).wait_recv()
        hand_y(n, u).start()

        @pl.when(gives_x)
        def _():
            hand_x(n, u).start()

        @pl.when(jnp.logical_or(i == 0, i == n_row - 1))
        def _():
            send_too(n, u).wait_recv()

        @pl.when(jnp.where(even, i == 0, i == n_row - 1))
        def _():
            hand_too(n, u, X).start()

        @pl.when(jnp.where(even, i == n_row - 1, i == 0))
        def _():
            hand_too(n, u, Z).start()

    def hand_third(n, u):
        hand_y(n, u).wait_recv()

        @pl.when(gives_z)
        def _():
            hand_z(n, u).start()

    def own_copy(n):
        return pltpu.make_async_copy(block(n, own), held.at[n, :, pl.ds(0, CHUNK)], own_sem.at[n])

    load_b(0).wait()
    for n in range(1, chunks):
        load_b(n).start()
    for m in range(tiles):
        load_a(m).start()
    mask_b(0)
    pl.semaphore_wait(barrier, len(near))
    for u in range(AHEAD):
        begin(0, u)
    for u in range(min(AHEAD + LEAD, PIECES)):
        begin_too(0, u)
    own_copy(0).start()
    for n in range(1, chunks):
        load_b(n).wait()
        mask_b(n)
        own_copy(n).start()
        for u in range(min(AHEAD + LEAD - n * PIECES, PIECES)):
            begin_too(n, u)

    fa[...] = lanes_expanded(af_ref[...], depth)
    size_a = rows // fa.shape[0]

    @pl.loop(0, tiles)
    def _(m):
        load_a(m).wait()

        @pl.loop(0, TILE // size_a)
        def _(k):
            part = pl.ds(pl.multiple_of(m * TILE + k * size_a, size_a), size_a)
            row = fa[pl.ds(m * (TILE // size_a) + k, 1), :].astype(jnp.bfloat16)
            left[part, :] = left[part, :] * row

    for n in range(chunks):
        own_copy(n).wait()

    partner = either(at(0, 1), at(0, -1))

    def x_copy(n, m):
        return remote(xs.at[n, m], xr.at[n, m], send_x.at[n, m], recv_x.at[n, m], partner)

    def q_copy(n, m):
        return remote(qs.at[n, m], qr.at[n, m], send_q.at[n, m], recv_q.at[n, m], at(0, -2))

    def z_copy(n, m):
        return remote(zs.at[n, m], zr.at[n, m], send_z.at[n, m], recv_z.at[n, m], either(at(0, -3), at(0, -1)))

    for u in range(LEAD):
        go_on_too(u // PIECES, u % PIECES)

    def product(n, m, first):
        part = pl.ds(pl.multiple_of(m * TILE, TILE), TILE)
        pair = held[n, :, first * CHUNK : (first + 2) * CHUNK]
        return jnp.dot(left[part, :], pair, preferred_element_type=jnp.float32)

    half_tiles = tiles // 2

    def first_pair(n, low, high):
        if low == 0:
            for u in range(PIECES):
                hand_x(n, u).wait_recv()

        @pl.loop(low, high)
        def _(m):
            value = product(n, m, X)
            xs[n, m] = value[:, :CHUNK]
            x_copy(n, m).start()
            kept[m] = value[:, CHUNK:]

    def first_end(n, low, high):
        @pl.loop(low, high)
        def _(m):
            x_copy(n, m).wait_recv()
            coded(kept[m] + xr[n, m], qs.at[n, m])
            q_copy(n, m).start()

    def second_pair(n, low, high):
        if low == 0:
            for u in range(PIECES):
                hand_z(n, u).wait_recv()

        @pl.loop(low, high)
        def _(m):
            value = product(n, m, OWN)
            acc[n, m] = value[:, :CHUNK]
            coded(value[:, CHUNK:], zs.at[n, m])
            z_copy(n, m).start()

    @pl.loop(0, chunks)
    def _(n):
        for u in range(PIECES):
            ahead, rest = divmod(u + AHEAD, PIECES)

            @pl.when(n + ahead < chunks)
            def _():
                begin(n + ahead, rest)

            later, rest_later = divmod(u + AHEAD + LEAD, PIECES)

            @pl.when(n + later < chunks)
            def _():
                begin_too(n + later, rest_later)

            soon, rest_soon = divmod(u + LEAD, PIECES)

            @pl.when(n + soon < chunks)
            def _():
                go_on_too(n + soon, rest_soon)

            hand_on(n, u)
            if u == 0:
                @pl.when(n > 0)
                def _():
                    hand_third(n - 1, PIECES - 1)
            else:
                hand_third(n, u - 1)
            if u == 0:
                @pl.when(n > 1)
                def _():
                    second_pair(n - 2, half_tiles, tiles)
            if u == 1:
                @pl.when(n > 0)
                def _():
                    first_pair(n - 1, 0, half_tiles)
            if u == 2:
                @pl.when(n > 0)
                def _():
                    first_pair(n - 1, half_tiles, tiles)
                    first_end(n - 1, 0, half_tiles)
            if u == 3:
                @pl.when(n > 0)
                def _():
                    first_end(n - 1, half_tiles, tiles)
                    second_pair(n - 1, 0, half_tiles)

    hand_third(chunks - 1, PIECES - 1)
    second_pair(chunks - 2, half_tiles, tiles)
    first_pair(chunks - 1, 0, tiles)
    first_end(chunks - 1, 0, tiles)
    second_pair(chunks - 1, 0, tiles)

    def store(n, m):
        where = o_ref.at[
            pl.ds(pl.multiple_of(m * TILE, TILE), TILE), pl.ds(pl.multiple_of(n * CHUNK, CHUNK), CHUNK)
        ]
        return pltpu.make_async_copy(acc.at[n, m], where, o_sem.at[n, m])

    @pl.loop(0, chunks)
    def _(n):
        @pl.loop(0, tiles)
        def _(m):
            q_copy(n, m).wait_recv()
            z_copy(n, m).wait_recv()
            for g in range(TILE // GROUP):
                part = pl.ds(g * GROUP, GROUP)
                acc[n, m, part, :] = acc[n, m, part, :] + decoded(qr.at[n, m], g) + decoded(zr.at[n, m], g)
            store(n, m).start()

    @pl.loop(0, chunks)
    def _(n):
        for u in range(PIECES):
            send_via(n, u).wait_send()
            hand_y(n, u).wait_send()

            @pl.when(gives_x)
            def _():
                hand_x(n, u).wait_send()

            @pl.when(gives_z)
            def _():
                hand_z(n, u).wait_send()

            @pl.when(sends_too)
            def _():
                send_too(n, u).wait_send()

            @pl.when(passes_too)
            def _():
                pass_too(n, u).wait_send()

        @pl.loop(0, tiles)
        def _(m):
            x_copy(n, m).wait_send()
            q_copy(n, m).wait_send()
            z_copy(n, m).wait_send()
            store(n, m).wait()


def per_device(n_row, n_col, a_panels, a_flags, b_panels, b_flags):
    rows, depth = a_panels.shape
    columns = b_panels.shape[1]
    chunks, tiles = columns // CHUNK, rows // TILE
    bf16, f32, dma = jnp.bfloat16, jnp.float32, pltpu.SemaphoreType.DMA
    tile = pltpu.VMEM((chunks, tiles, TILE, CHUNK), f32)
    code = pltpu.VMEM((chunks, tiles, TILE // GROUP * (GROUP + PAD), CHUNK), jnp.int16)
    each = dma((chunks, tiles))
    return pl.pallas_call(
        functools.partial(kernel, n_row, n_col),
        name="block_products",
        out_shape=jax.ShapeDtypeStruct((rows, columns), f32),
        in_specs=[
            pl.BlockSpec(memory_space=pl.ANY),
            pl.BlockSpec(memory_space=pltpu.VMEM),
            pl.BlockSpec(memory_space=pl.ANY),
            pl.BlockSpec(memory_space=pltpu.VMEM),
        ],
        out_specs=pl.BlockSpec(memory_space=pl.ANY),
        scratch_shapes=[
            pltpu.VMEM((rows, depth), bf16),
            pltpu.VMEM((chunks, b_panels.shape[0], CHUNK), bf16),
            pltpu.VMEM((a_flags.shape[0], depth), f32),
            pltpu.VMEM((b_flags.shape[0], columns), f32),
            pltpu.VMEM((chunks, depth, 4 * CHUNK), bf16),
            pltpu.VMEM((chunks, depth, CHUNK), bf16),
            pltpu.VMEM((chunks, depth, CHUNK), bf16),
            pltpu.VMEM((tiles, TILE, CHUNK), f32),
            tile, tile, tile,
            code, code, code, code,
            dma((tiles,)), dma((chunks,)), dma((chunks,)), each,
            dma((7, chunks, PIECES)), dma((6, chunks, PIECES)),
            each, each, each, each, each, each,
        ],
        compiler_params=pltpu.CompilerParams(
            collective_id=0, has_side_effects=True, vmem_limit_bytes=60 * 2**20
        ),
        cost_estimate=pl.CostEstimate(
            flops=8 * rows * depth * columns, bytes_accessed=2 * rows * depth + 8 * rows * columns, transcendentals=0
        ),
    )(a_panels, a_flags, b_panels, b_flags.T)


def solution(mesh):
    placed = (P("row", "col"), P("row", "col"), P("row", "col"), P("row", "col"))
    return jax.shard_map(
        functools.partial(per_device, mesh.shape["row"], mesh.shape["col"]),
        mesh=mesh, in_specs=placed, out_specs=P("row", "col"), check_vma=False,
    )
```
